32 devices in a mesh: outer: 4 (over y, x), inner: 8 (over z, core).
Axes of the slice: x: 2, y: 2, z: 4, core: 2. Of those that a mesh axis runs over, the one named last changes fastest.
Arguments:
- queries: bfloat16 [8192, 2048], P(('outer', 'inner')), may hold values from -4 to 4
- key_rows: bfloat16 [8192, 128], P(('outer', 'inner')), may hold values from -4 to 4
- value_rows: bfloat16 [8192, 128], P(('outer', 'inner')), may hold values from -6 to 6
- out_grad: bfloat16 [8192, 2048], P(('outer', 'inner')), may hold values from -96 to 96
- outputs: bfloat16 [8192, 2048], P(('outer', 'inner')), may hold values from -1.75 to 1.75
- log_sum: float32 [16, 8192], P(None, ('outer', 'inner')), may hold values from 6 to 7.5
- span_table: int32 [32, 2], replicated, may hold values from 0 to 63, as said below
Outputs:
- query_grad: bfloat16 [8192, 2048], P(('outer', 'inner'))
- key_grad: float32 [8192, 128], P(('outer', 'inner'))
- value_grad: float32 [8192, 128], P(('outer', 'inner'))
The draws below stay inside these ranges and needn't reach their ends.
Inputs may be any that keep to these rules, and one draw needn't show every extreme that they name: `span_table`: row e holds spans p and 63 - p, where p over the rows is a permutation of 0 to 31.
All inputs are finite; a program needn't handle non-finite values.
Results may differ from the reference program's by a relative error of at most 0.0075.
Values may be sent and summed in bfloat16 or wider, within the bound.
A program may use at most 64 MiB of HBM per device.

```python
import math
import jax
import jax.numpy as jnp
from jax import lax

HD = 128
GROUP = 16
SPAN = 128
OUT_STEPS = 2
IN_STEPS = 2
SPANS = 64
SEQ = 8192
N_OUTER = 4
N_INNER = 8


def draw_span_table(key, part):
    key = jax.random.fold_in(key, 11)
    leading = jax.random.permutation(key, SPANS // 2).astype(jnp.int32)
    return jnp.stack([leading, SPANS - 1 - leading], axis=1).astype(jnp.int32)


def shard_levels(stream_key, shape, shards, low, largest):
    def one(dim, shards_of):
        steps = jax.random.uniform(jax.random.fold_in(jax.random.fold_in(stream_key, 6), dim), (shards_of,), jnp.float32, low / len(shards), largest / len(shards))
        return jnp.repeat(jnp.exp(steps), shape[dim] // shards_of).reshape((-1,) + (1,) * (len(shape) - dim - 1))

    factor_of = one(*shards[0])
    for cut in shards[1:]:
        factor_of = factor_of * one(*cut)
    return factor_of


def normal_values(key, extent, deviation, most, pieces=(), kind=jnp.bfloat16):
    factor_of = shard_levels(key, extent, pieces, -0.22, 0.18) if pieces else 1.0
    result = jax.random.normal(key, extent, jnp.float32) * deviation * factor_of
    return jnp.minimum(jnp.maximum(result, -most), most).astype(kind)


def setup_inputs(seed: int = 0) -> dict:
    splits = jax.random.split(jax.random.key(seed), 8)
    return {
        "queries": normal_values(splits[0], (SEQ, GROUP * HD), 1.0, 4.0, ((0, 32),)),
        "key_rows": normal_values(splits[1], (SEQ, HD), 1.0, 4.0, ((0, 32),)),
        "value_rows": normal_values(splits[2], (SEQ, HD), 1.0, 6.0, ((0, 32),)),
        "out_grad": normal_values(splits[3], (SEQ, GROUP * HD), 16.0, 96.0, ((0, 32),)),
        "outputs": normal_values(splits[4], (SEQ, GROUP * HD), 0.3, 1.75, ((0, 32),)),
        "log_sum": jnp.clip(6.0 + 1.5 * jax.random.uniform(splits[5], (GROUP, SEQ), jnp.float32) ** shard_levels(splits[5], (GROUP, SEQ), ((1, 32),), -0.2, 0.2), 6.0, 7.5),
        "span_table": draw_span_table(jax.random.fold_in(splits[7], 71), 0),
    }


def rounded(values):
    return lax.optimization_barrier(values.astype(jnp.bfloat16)).astype(jnp.float32)

def block_grads(query_block, key_block, value_block, grad_block, log_block, row_dot, query_pos, key_pos, factor):
    query_wide = query_block.astype(jnp.float32)
    key_wide = key_block.astype(jnp.float32)
    value_wide = value_block.astype(jnp.float32)
    grad_wide = grad_block.astype(jnp.float32)
    scores = jnp.einsum('qgd,kd->gqk', query_wide, key_wide) * factor
    visible = key_pos[None, None, :] <= query_pos[None, :, None]
    weights = jnp.where(visible, jnp.exp(scores - log_block[:, :, None]), 0.0)
    dweights = jnp.einsum('qgd,kd->gqk', grad_wide, value_wide)
    dscores = weights * (dweights - row_dot[:, :, None])
    weights_low = rounded(weights)
    dscores_low = rounded(dscores)
    value_part = jnp.einsum('gqk,qgd->kd', weights_low, grad_wide)
    key_part = jnp.einsum('gqk,qgd->kd', dscores_low, query_wide)
    query_part = jnp.einsum('gqk,kd->qgd', dscores_low, key_wide)
    return (query_part, key_part, value_part)

def reference(queries, key_rows, value_rows, out_grad, outputs, log_sum, span_table):
    block_count = N_OUTER * N_INNER
    row_count = 2 * SPAN
    factor = 1.0 / math.sqrt(HD)
    query_all = queries.reshape(block_count, row_count, GROUP, HD)
    grad_all = out_grad.reshape(block_count, row_count, GROUP, HD)
    output_all = outputs.reshape(block_count, row_count, GROUP, HD)
    key_all = key_rows.reshape(block_count, row_count, HD)
    value_all = value_rows.reshape(block_count, row_count, HD)
    log_all = log_sum.reshape(GROUP, block_count, row_count).transpose(1, 0, 2)
    offsets = jnp.arange(SPAN, dtype=jnp.int32)
    positions = (span_table[:, :, None] * SPAN + offsets[None, None, :]).reshape(block_count, row_count)

    def per_block(block_index):
        outer_index = block_index // N_INNER
        inner_index = block_index % N_INNER
        query_block = query_all[block_index]
        grad_block = grad_all[block_index]
        row_dot = lax.optimization_barrier(jnp.sum(grad_block.astype(jnp.float32) * output_all[block_index].astype(jnp.float32), axis=-1)).T
        log_block = log_all[block_index]
        query_pos = positions[block_index]
        query_total = jnp.zeros((row_count, GROUP, HD), jnp.float32)
        key_parts = []
        value_parts = []
        for a in range(OUT_STEPS):
            for b in range(IN_STEPS):
                source = ((outer_index - a) % N_OUTER * N_INNER + (inner_index - b) % N_INNER).astype(jnp.int32)
                query_part, key_part, value_part = block_grads(query_block, key_all[source], value_all[source], grad_block, log_block, row_dot, query_pos, positions[source], factor)
                query_total = query_total + query_part
                key_parts.append(key_part)
                value_parts.append(value_part)
        query_out = (query_total * factor).astype(jnp.bfloat16).reshape(row_count, GROUP * HD)
        return (query_out, jnp.stack(key_parts), jnp.stack(value_parts))
    query_out, key_stack, value_stack = lax.map(per_block, jnp.arange(block_count, dtype=jnp.int32))
    key_stack = key_stack.reshape(N_OUTER, N_INNER, OUT_STEPS * IN_STEPS, row_count, HD)
    value_stack = value_stack.reshape(N_OUTER, N_INNER, OUT_STEPS * IN_STEPS, row_count, HD)
    key_total = jnp.zeros((N_OUTER, N_INNER, row_count, HD), jnp.float32)
    value_total = jnp.zeros((N_OUTER, N_INNER, row_count, HD), jnp.float32)
    for a in range(OUT_STEPS):
        for b in range(IN_STEPS):
            step = a * IN_STEPS + b
            key_total = key_total + jnp.roll(key_stack[:, :, step], (-a, -b), axis=(0, 1))
            value_total = value_total + jnp.roll(value_stack[:, :, step], (-a, -b), axis=(0, 1))
    key_grad = (key_total * factor).reshape(SEQ, HD)
    value_grad = value_total.reshape(SEQ, HD)
    return (query_out.reshape(SEQ, GROUP * HD), key_grad, value_grad)
```

```python
import functools
import math

import jax
import jax.numpy as jnp
from jax import lax
from jax.experimental import pallas as pl
from jax.experimental.pallas import tpu as pltpu
from jax.sharding import PartitionSpec as P

MESH = pl.DeviceIdType.MESH
HD = 128
LOG2E = 1.4426950408889634
F32 = jnp.float32
BF16 = jnp.bfloat16

STEPS = ((0, 1), (1, 0), (1, 1))
SEND_ORDER = (1, 2, 0)


def dot_nt(a, b):
    return lax.dot_general(a, b, (((1,), (1,)), ((), ())), preferred_element_type=F32)


def dot(a, b):
    return jnp.dot(a, b, preferred_element_type=F32)


def kernel(
    outer_count, inner_count, heads,
    span_ref, q_hbm, k_hbm, v_hbm, do_hbm, o_hbm, lse_hbm,
    dq_hbm, dk_ref, dv_ref,
    q, do, o, own_k, own_v, lse, lse2, rdot,
    kin_a, kin_b, kin_c, vin_a, vin_b, vin_c, pin, pout, p_t, ds_t, dq_l, dq_stage,
    in_sem, ks_send, ks_recv, vs_send, vs_recv, ps_send, ps_recv, out_sem,
):
    me_o = lax.axis_index("outer")
    me_i = lax.axis_index("inner")
    pairs = heads // 2
    factor = 1.0 / math.sqrt(HD)
    kin, vin = (kin_a, kin_b, kin_c), (vin_a, vin_b, vin_c)

    loads = [
        pltpu.make_async_copy(src, dst, in_sem.at[n])
        for n, (src, dst) in enumerate(
            ((lse_hbm, lse), (k_hbm, own_k), (v_hbm, own_v), (do_hbm, do), (o_hbm, o), (q_hbm, q))
        )
    ]
    for load in loads:
        load.start()

    def ahead(step):
        return (lax.rem(me_o + step[0], outer_count), lax.rem(me_i + step[1], inner_count))

    def behind(step):
        return (
            lax.rem(me_o + outer_count - step[0], outer_count),
            lax.rem(me_i + inner_count - step[1], inner_count),
        )

    barrier = pltpu.get_barrier_semaphore()
    for step in STEPS:
        pl.semaphore_signal(barrier, inc=1, device_id=ahead(step), device_id_type=MESH)
        pl.semaphore_signal(barrier, inc=1, device_id=behind(step), device_id_type=MESH)
    pl.semaphore_wait(barrier, 2 * len(STEPS))

    k_copies, v_copies = {}, {}
    for j in SEND_ORDER:
        for table, src, dst, ssem, rsem in (
            (k_copies, k_hbm, kin, ks_send, ks_recv),
            (v_copies, v_hbm, vin, vs_send, vs_recv),
        ):
            table[j] = pltpu.make_async_remote_copy(
                src_ref=src, dst_ref=dst[j], send_sem=ssem.at[j], recv_sem=rsem.at[j],
                device_id=ahead(STEPS[j]), device_id_type=MESH,
            )
            table[j].start()

    def cols(h):
        return slice(h * HD, (h + 1) * HD)

    def pair_rows(ref, half, p):
        return jnp.concatenate([ref[half, :, cols(2 * p)], ref[half, :, cols(2 * p + 1)]], axis=0)

    def all_rows(ref, half):
        return jnp.concatenate([ref[half, :, cols(h)] for h in range(heads)], axis=0)

    def pair_lanes(ref, half, p):
        return jnp.concatenate(
            [ref[half, 2 * p : 2 * p + 1, :], ref[half, 2 * p + 1 : 2 * p + 2, :]], axis=1
        )

    for load in loads[:5]:
        load.wait()
    for s in range(2):
        lse2[s] = lse[:, s * HD : (s + 1) * HD] * LOG2E
    ones = jnp.ones((16, 2 * HD), BF16)
    for s in range(2):
        for p in range(pairs):
            terms = []
            for h in (2 * p, 2 * p + 1):
                prod = do[s, :, cols(h)].astype(F32) * o[s, :, cols(h)].astype(F32)
                high = prod.astype(BF16)
                low = (prod - high.astype(F32)).astype(BF16)
                terms.append(jnp.concatenate([high, low], axis=1))
            sums = dot_nt(ones, jnp.concatenate(terms, axis=0))
            rdot[s, 2 * p : 2 * p + 1, :] = sums[0:1, :HD]
            rdot[s, 2 * p + 1 : 2 * p + 2, :] = sums[0:1, HD:]
    loads[5].wait()

    scale2 = factor * LOG2E

    def weights(keys, values, half, p, mask):
        scores = dot_nt(keys, pair_rows(q, half, p))
        dprobs = dot_nt(values, pair_rows(do, half, p))
        probs = jnp.exp2(scores * scale2 - pair_lanes(lse2, half, p))
        if mask is not None:
            probs = jnp.where(mask, probs, 0.0)
        dscores = probs * (dprobs - pair_lanes(rdot, half, p))
        return probs.astype(BF16), dscores.astype(BF16)

    k_rows = lax.broadcasted_iota(jnp.int32, (HD, 2 * HD), 0)
    q_lanes = lax.broadcasted_iota(jnp.int32, (HD, 2 * HD), 1) % HD
    triangle = k_rows <= q_lanes
    lo_k, hi_k = own_k[0], own_k[1]
    lo_v, hi_v = own_v[0], own_v[1]
    for p in range(pairs):
        lanes = slice(2 * p * HD, (2 * p + 2) * HD)
        for row, keys, values, half, mask in (
            (0, lo_k, lo_v, 0, triangle), (1, lo_k, lo_v, 1, None), (2, hi_k, hi_v, 1, triangle)
        ):
            probs, dscores = weights(keys, values, half, p, mask)
            p_t[row * HD : (row + 1) * HD, lanes] = probs
            ds_t[row * HD : (row + 1) * HD, lanes] = dscores
    for out, lhs, rhs in ((dv_ref, p_t, do), (dk_ref, ds_t, q)):
        late = dot(lhs[HD : 3 * HD, :], all_rows(rhs, 1))
        out[0] = late[:HD] + dot(lhs[:HD, :], all_rows(rhs, 0))
        out[1] = late[HD:]

    zero = jnp.zeros((HD, HD), BF16)
    dq_l[0:HD, 0:HD] = zero
    dq_l[HD:, 0:HD] = lo_k.T
    dq_l[0:HD, HD : 2 * HD] = lo_k.T
    dq_l[0:HD, 2 * HD : 3 * HD] = hi_k.T
    dq_l[HD:, HD : 2 * HD] = zero
    dq_l[HD:, 2 * HD : 3 * HD] = zero

    me_span = span_ref[0, me_o * inner_count + me_i]
    p_copies = []
    for j, step in enumerate(STEPS):
        src_o, src_i = behind(step)
        src_span = span_ref[0, src_o * inner_count + src_i]
        early = src_span < me_span
        half = jnp.where(early, 0, 1)
        k_copies[j].wait_recv()
        v_copies[j].wait_recv()
        lo_k, sel_k = kin[j][0], kin[j][half]
        lo_v, sel_v = vin[j][0], vin[j][half]
        base = (3 + 2 * j) * HD
        for p in range(pairs):
            lanes = slice(2 * p * HD, (2 * p + 2) * HD)
            for row, keys, values, side in ((0, lo_k, lo_v, 1), (1, sel_k, sel_v, half)):
                probs, dscores = weights(keys, values, side, p, None)
                p_t[row * HD : (row + 1) * HD, lanes] = probs
                ds_t[base + row * HD : base + (row + 1) * HD, lanes] = dscores
        is_early = jnp.full((HD, HD), src_span, jnp.int32) < me_span
        for n, (lhs, at, rhs) in enumerate(((ds_t, base, q), (p_t, 0, do))):
            on_lo = dot(lhs[at : at + HD, :], all_rows(rhs, 1))
            on_sel = dot(lhs[at + HD : at + 2 * HD, :], all_rows(rhs, half))
            pout[j, 2 * n] = (on_lo + jnp.where(is_early, on_sel, 0.0)).astype(BF16)
            pout[j, 2 * n + 1] = jnp.where(is_early, 0.0, on_sel).astype(BF16)
        copy = pltpu.make_async_remote_copy(
            src_ref=pout.at[j], dst_ref=pin.at[j], send_sem=ps_send.at[j], recv_sem=ps_recv.at[j],
            device_id=behind(step), device_id_type=MESH,
        )
        copy.start()
        p_copies.append(copy)
        sel_t = sel_k.astype(F32).T
        dq_l[0:HD, base : base + HD] = lo_k.T
        dq_l[0:HD, base + HD : base + 2 * HD] = jnp.where(is_early, 0.0, sel_t).astype(BF16)
        dq_l[HD:, base : base + HD] = zero
        dq_l[HD:, base + HD : base + 2 * HD] = jnp.where(is_early, sel_t, 0.0).astype(BF16)

    stores = []
    for p in range(pairs):
        lanes = slice(2 * p * HD, (2 * p + 2) * HD)
        grads = dot(dq_l[...], ds_t[:, lanes]) * factor
        for s in range(2):
            for n in range(2):
                tile = grads[(1 - s) * HD : (2 - s) * HD, n * HD : (n + 1) * HD]
                dq_stage[s, :, cols(2 * p + n)] = tile.T.astype(BF16)
        store = pltpu.make_async_copy(
            dq_stage.at[:, :, lanes], dq_hbm.at[:, :, lanes], out_sem.at[p]
        )
        store.start()
        stores.append(store)

    for j in range(len(STEPS)):
        p_copies[j].wait_recv()
    for s in range(2):
        dk_ref[s] = (dk_ref[s] + sum(pin[j, s].astype(F32) for j in range(len(STEPS)))) * factor
        dv_ref[s] = dv_ref[s] + sum(pin[j, 2 + s].astype(F32) for j in range(len(STEPS)))
    for store in stores:
        store.wait()
    for j in range(len(STEPS)):
        k_copies[j].wait_send()
        v_copies[j].wait_send()
        p_copies[j].wait_send()


def per_device(outer_count, inner_count, queries, key_rows, value_rows, out_grad, outputs, log_sum, span_table):
    heads = log_sum.shape[0]
    rows, width = queries.shape
    half = rows // 2
    steps = len(STEPS)
    any_spec = pl.BlockSpec(memory_space=pl.ANY)
    vmem = pl.BlockSpec(memory_space=pltpu.VMEM)
    smem = pl.BlockSpec(memory_space=pltpu.SMEM)
    wide = (2, half, width)
    narrow = (2, half, HD)
    dma = pltpu.SemaphoreType.DMA
    dq, dk, dv = pl.pallas_call(
        functools.partial(kernel, outer_count, inner_count, heads),
        out_shape=(
            jax.ShapeDtypeStruct(wide, BF16),
            jax.ShapeDtypeStruct(narrow, F32),
            jax.ShapeDtypeStruct(narrow, F32),
        ),
        in_specs=[smem] + [any_spec] * 6,
        out_specs=(any_spec, vmem, vmem),
        scratch_shapes=[
            pltpu.VMEM(wide, BF16), pltpu.VMEM(wide, BF16), pltpu.VMEM(wide, BF16),
            pltpu.VMEM(narrow, BF16), pltpu.VMEM(narrow, BF16),
            pltpu.VMEM((heads, rows), F32), pltpu.VMEM((2, heads, half), F32), pltpu.VMEM((2, heads, half), F32),
            *[pltpu.VMEM(narrow, BF16) for _ in range(2 * steps)],
            pltpu.VMEM((steps, 4, half, HD), BF16), pltpu.VMEM((steps, 4, half, HD), BF16),
            pltpu.VMEM((3 * half, width), BF16),
            pltpu.VMEM(((3 + 2 * steps) * half, width), BF16),
            pltpu.VMEM((2 * HD, (3 + 2 * steps) * half), BF16),
            pltpu.VMEM(wide, BF16),
            dma((6,)), dma((steps,)), dma((steps,)), dma((steps,)), dma((steps,)),
            dma((steps,)), dma((steps,)), dma((heads // 2,)),
        ],
        compiler_params=pltpu.CompilerParams(
            collective_id=0, has_side_effects=True, vmem_limit_bytes=60 * 1024 * 1024
        ),
        cost_estimate=pl.CostEstimate(
            flops=2 * 5 * 9 * heads * half * half * HD, bytes_accessed=4 * rows * width * 2,
            transcendentals=9 * heads * half * half,
        ),
    )(
        span_table.T, queries.reshape(wide), key_rows.reshape(narrow), value_rows.reshape(narrow),
        out_grad.reshape(wide), outputs.reshape(wide), log_sum,
    )
    return dq.reshape(rows, width), dk.reshape(rows, HD), dv.reshape(rows, HD)


def solution(mesh):
    rows = P(("outer", "inner"), None)
    return jax.shard_map(
        functools.partial(per_device, mesh.shape["outer"], mesh.shape["inner"]),
        mesh=mesh,
        in_specs=(rows, rows, rows, rows, rows, P(None, ("outer", "inner")), P()),
        out_specs=(rows, rows, rows),
        check_vma=False,
    )
```

```python
import functools
import math

import jax
import jax.numpy as jnp
from jax import lax
from jax.experimental import pallas as pl
from jax.experimental.pallas import tpu as pltpu
from jax.sharding import PartitionSpec as P

MESH = pl.DeviceIdType.MESH
HD = 128
LOG2E = 1.4426950408889634
F32 = jnp.float32
BF16 = jnp.bfloat16

STEPS = ((0, 1), (1, 0), (1, 1))
SEND_ORDER = (1, 2, 0)


def dot_nt(a, b):
    return lax.dot_general(a, b, (((1,), (1,)), ((), ())), preferred_element_type=F32)


def dot(a, b):
    return jnp.dot(a, b, preferred_element_type=F32)


def kernel(
    outer_count, inner_count, heads,
    span_ref, q_hbm, k_hbm, v_hbm, do_hbm, o_hbm, lse_hbm,
    dq_hbm, dk_ref, dv_ref,
    q, do, o, q_t, do_t, own_k, own_v, lse, lse2, rdot,
    kin_a, kin_b, kin_c, vin_a, vin_b, vin_c, pin, pout, p_t, ds_t, dq_l, dq_stage,
    in_sem, ks_send, ks_recv, vs_send, vs_recv, ps_send, ps_recv, out_sem,
):
    me_o = lax.axis_index("outer")
    me_i = lax.axis_index("inner")
    pairs = heads // 2
    factor = 1.0 / math.sqrt(HD)
    kin, vin = (kin_a, kin_b, kin_c), (vin_a, vin_b, vin_c)

    loads = [
        pltpu.make_async_copy(src, dst, in_sem.at[n])
        for n, (src, dst) in enumerate(
            ((lse_hbm, lse), (k_hbm, own_k), (v_hbm, own_v), (do_hbm, do), (o_hbm, o), (q_hbm, q))
        )
    ]
    for load in loads:
        load.start()

    def ahead(step):
        return (lax.rem(me_o + step[0], outer_count), lax.rem(me_i + step[1], inner_count))

    def behind(step):
        return (
            lax.rem(me_o + outer_count - step[0], outer_count),
            lax.rem(me_i + inner_count - step[1], inner_count),
        )

    barrier = pltpu.get_barrier_semaphore()
    for step in STEPS:
        pl.semaphore_signal(barrier, inc=1, device_id=ahead(step), device_id_type=MESH)
        pl.semaphore_signal(barrier, inc=1, device_id=behind(step), device_id_type=MESH)
    pl.semaphore_wait(barrier, 2 * len(STEPS))

    k_copies, v_copies = {}, {}
    for j in SEND_ORDER:
        for table, src, dst, ssem, rsem in (
            (k_copies, k_hbm, kin, ks_send, ks_recv),
            (v_copies, v_hbm, vin, vs_send, vs_recv),
        ):
            table[j] = pltpu.make_async_remote_copy(
                src_ref=src, dst_ref=dst[j], send_sem=ssem.at[j], recv_sem=rsem.at[j],
                device_id=ahead(STEPS[j]), device_id_type=MESH,
            )
            table[j].start()

    def cols(h):
        return slice(h * HD, (h + 1) * HD)

    def all_rows(ref, half):
        return jnp.concatenate([ref[half, :, cols(h)] for h in range(heads)], axis=0)

    def pair_lanes(ref, half, p):
        return jnp.concatenate(
            [ref[half, 2 * p : 2 * p + 1, :], ref[half, 2 * p + 1 : 2 * p + 2, :]], axis=1
        )

    for load in loads[:5]:
        load.wait()
    for s in range(2):
        lse2[s] = lse[:, s * HD : (s + 1) * HD] * LOG2E
    ones = jnp.ones((16, 2 * HD), BF16)
    for s in range(2):
        for p in range(pairs):
            terms = []
            for h in (2 * p, 2 * p + 1):
                prod = do[s, :, cols(h)].astype(F32) * o[s, :, cols(h)].astype(F32)
                high = prod.astype(BF16)
                low = (prod - high.astype(F32)).astype(BF16)
                terms.append(jnp.concatenate([high, low], axis=1))
            sums = dot_nt(ones, jnp.concatenate(terms, axis=0))
            rdot[s, 2 * p : 2 * p + 1, :] = sums[0:1, :HD]
            rdot[s, 2 * p + 1 : 2 * p + 2, :] = sums[0:1, HD:]
    loads[5].wait()
    for s in range(2):
        for h in range(heads):
            q_t[s, :, cols(h)] = q[s, :, cols(h)].T
            do_t[s, :, cols(h)] = do[s, :, cols(h)].T

    scale2 = factor * LOG2E

    def weights(keys, values, half, p, mask):
        lanes = slice(2 * p * HD, (2 * p + 2) * HD)
        scores = dot(keys, q_t[half, :, lanes])
        dprobs = dot(values, do_t[half, :, lanes])
        probs = jnp.exp2(scores * scale2 - pair_lanes(lse2, half, p))
        if mask is not None:
            probs = jnp.where(mask, probs, 0.0)
        dscores = probs * (dprobs - pair_lanes(rdot, half, p))
        return probs.astype(BF16), dscores.astype(BF16)

    k_rows = lax.broadcasted_iota(jnp.int32, (HD, 2 * HD), 0)
    q_lanes = lax.broadcasted_iota(jnp.int32, (HD, 2 * HD), 1) % HD
    triangle = k_rows <= q_lanes
    lo_k, hi_k = own_k[0], own_k[1]
    lo_v, hi_v = own_v[0], own_v[1]
    for p in range(pairs):
        lanes = slice(2 * p * HD, (2 * p + 2) * HD)
        for row, keys, values, half, mask in (
            (0, lo_k, lo_v, 0, triangle), (1, lo_k, lo_v, 1, None), (2, hi_k, hi_v, 1, triangle)
        ):
            probs, dscores = weights(keys, values, half, p, mask)
            p_t[row * HD : (row + 1) * HD, lanes] = probs
            ds_t[row * HD : (row + 1) * HD, lanes] = dscores
    for out, lhs, rhs in ((dv_ref, p_t, do), (dk_ref, ds_t, q)):
        late = dot(lhs[HD : 3 * HD, :], all_rows(rhs, 1))
        out[0] = late[:HD] + dot(lhs[:HD, :], all_rows(rhs, 0))
        out[1] = late[HD:]

    zero = jnp.zeros((HD, HD), BF16)
    dq_l[0:HD, 0:HD] = zero
    dq_l[HD:, 0:HD] = lo_k.T
    dq_l[0:HD, HD : 2 * HD] = lo_k.T
    dq_l[0:HD, 2 * HD : 3 * HD] = hi_k.T
    dq_l[HD:, HD : 2 * HD] = zero
    dq_l[HD:, 2 * HD : 3 * HD] = zero

    me_span = span_ref[0, me_o * inner_count + me_i]
    p_copies = []
    for j, step in enumerate(STEPS):
        src_o, src_i = behind(step)
        src_span = span_ref[0, src_o * inner_count + src_i]
        early = src_span < me_span
        half = jnp.where(early, 0, 1)
        k_copies[j].wait_recv()
        v_copies[j].wait_recv()
        lo_k, sel_k = kin[j][0], kin[j][half]
        lo_v, sel_v = vin[j][0], vin[j][half]
        base = (3 + 2 * j) * HD
        for p in range(pairs):
            lanes = slice(2 * p * HD, (2 * p + 2) * HD)
            for row, keys, values, side in ((0, lo_k, lo_v, 1), (1, sel_k, sel_v, half)):
                probs, dscores = weights(keys, values, side, p, None)
                p_t[row * HD : (row + 1) * HD, lanes] = probs
                ds_t[base + row * HD : base + (row + 1) * HD, lanes] = dscores
        is_early = jnp.full((HD, HD), src_span, jnp.int32) < me_span
        for n, (lhs, at, rhs) in enumerate(((ds_t, base, q), (p_t, 0, do))):
            on_lo = dot(lhs[at : at + HD, :], all_rows(rhs, 1))
            on_sel = dot(lhs[at + HD : at + 2 * HD, :], all_rows(rhs, half))
            pout[j, 2 * n] = (on_lo + jnp.where(is_early, on_sel, 0.0)).astype(BF16)
            pout[j, 2 * n + 1] = jnp.where(is_early, 0.0, on_sel).astype(BF16)
        copy = pltpu.make_async_remote_copy(
            src_ref=pout.at[j], dst_ref=pin.at[j], send_sem=ps_send.at[j], recv_sem=ps_recv.at[j],
            device_id=behind(step), device_id_type=MESH,
        )
        copy.start()
        p_copies.append(copy)
        sel_t = sel_k.astype(F32).T
        dq_l[0:HD, base : base + HD] = lo_k.T
        dq_l[0:HD, base + HD : base + 2 * HD] = jnp.where(is_early, 0.0, sel_t).astype(BF16)
        dq_l[HD:, base : base + HD] = zero
        dq_l[HD:, base + HD : base + 2 * HD] = jnp.where(is_early, sel_t, 0.0).astype(BF16)

    stores = []
    for p in range(pairs):
        lanes = slice(2 * p * HD, (2 * p + 2) * HD)
        grads = dot(dq_l[...], ds_t[:, lanes]) * factor
        for s in range(2):
            for n in range(2):
                tile = grads[(1 - s) * HD : (2 - s) * HD, n * HD : (n + 1) * HD]
                dq_stage[s, :, cols(2 * p + n)] = tile.T.astype(BF16)
        store = pltpu.make_async_copy(
            dq_stage.at[:, :, lanes], dq_hbm.at[:, :, lanes], out_sem.at[p]
        )
        store.start()
        stores.append(store)

    for j in range(len(STEPS)):
        p_copies[j].wait_recv()
    for s in range(2):
        dk_ref[s] = (dk_ref[s] + sum(pin[j, s].astype(F32) for j in range(len(STEPS)))) * factor
        dv_ref[s] = dv_ref[s] + sum(pin[j, 2 + s].astype(F32) for j in range(len(STEPS)))
    for store in stores:
        store.wait()
    for j in range(len(STEPS)):
        k_copies[j].wait_send()
        v_copies[j].wait_send()
        p_copies[j].wait_send()


def place(dq, dk, dv, dq_out, dk_out, dv_out, sem):
    copies = [
        pltpu.make_async_copy(src, dst, sem.at[n])
        for n, (src, dst) in enumerate(((dq, dq_out), (dk, dk_out), (dv, dv_out)))
    ]
    for copy in copies:
        copy.start()
    for copy in copies:
        copy.wait()


def per_device(outer_count, inner_count, queries, key_rows, value_rows, out_grad, outputs, log_sum, span_table):
    heads = log_sum.shape[0]
    rows, width = queries.shape
    half = rows // 2
    steps = len(STEPS)
    any_spec = pl.BlockSpec(memory_space=pl.ANY)
    vmem = pl.BlockSpec(memory_space=pltpu.VMEM)
    smem = pl.BlockSpec(memory_space=pltpu.SMEM)
    wide = (2, half, width)
    narrow = (2, half, HD)
    dma = pltpu.SemaphoreType.DMA
    dq, dk, dv = pl.pallas_call(
        functools.partial(kernel, outer_count, inner_count, heads),
        out_shape=(
            jax.ShapeDtypeStruct(wide, BF16),
            jax.ShapeDtypeStruct(narrow, F32),
            jax.ShapeDtypeStruct(narrow, F32),
        ),
        in_specs=[smem] + [pl.BlockSpec(memory_space=pltpu.HBM)] * 6,
        out_specs=(any_spec, vmem, vmem),
        scratch_shapes=[
            *[pltpu.VMEM(wide, BF16) for _ in range(5)],
            pltpu.VMEM(narrow, BF16), pltpu.VMEM(narrow, BF16),
            pltpu.VMEM((heads, rows), F32), pltpu.VMEM((2, heads, half), F32), pltpu.VMEM((2, heads, half), F32),
            *[pltpu.VMEM(narrow, BF16) for _ in range(2 * steps)],
            pltpu.VMEM((steps, 4, half, HD), BF16), pltpu.VMEM((steps, 4, half, HD), BF16),
            pltpu.VMEM((3 * half, width), BF16),
            pltpu.VMEM(((3 + 2 * steps) * half, width), BF16),
            pltpu.VMEM((2 * HD, (3 + 2 * steps) * half), BF16),
            pltpu.VMEM(wide, BF16),
            dma((6,)), dma((steps,)), dma((steps,)), dma((steps,)), dma((steps,)),
            dma((steps,)), dma((steps,)), dma((heads // 2,)),
        ],
        compiler_params=pltpu.CompilerParams(
            collective_id=0, has_side_effects=True, vmem_limit_bytes=60 * 1024 * 1024
        ),
        cost_estimate=pl.CostEstimate(
            flops=2 * 5 * 9 * heads * half * half * HD, bytes_accessed=4 * rows * width * 2,
            transcendentals=9 * heads * half * half,
        ),
    )(
        span_table.T, queries.reshape(wide), key_rows.reshape(narrow), value_rows.reshape(narrow),
        out_grad.reshape(wide), outputs.reshape(wide), log_sum,
    )
    dq, dk, dv = pl.pallas_call(
        place,
        out_shape=(
            jax.ShapeDtypeStruct(wide, BF16),
            jax.ShapeDtypeStruct(narrow, F32),
            jax.ShapeDtypeStruct(narrow, F32),
        ),
        in_specs=[any_spec] * 3,
        out_specs=[any_spec] * 3,
        scratch_shapes=[dma((3,))],
        compiler_params=pltpu.CompilerParams(vmem_limit_bytes=60 * 1024 * 1024),
    )(dq, dk, dv)
    return dq.reshape(rows, width), dk.reshape(rows, HD), dv.reshape(rows, HD)


def solution(mesh):
    rows = P(("outer", "inner"), None)
    return jax.shard_map(
        functools.partial(per_device, mesh.shape["outer"], mesh.shape["inner"]),
        mesh=mesh,
        in_specs=(rows, rows, rows, rows, rows, P(None, ("outer", "inner")), P()),
        out_specs=(rows, rows, rows),
        check_vma=False,
    )
```

```python
import functools
import math

import jax
import jax.numpy as jnp
from jax import lax
from jax.experimental import pallas as pl
from jax.experimental.pallas import tpu as pltpu
from jax.sharding import PartitionSpec as P

MESH = pl.DeviceIdType.MESH
HD = 128
LOG2E = 1.4426950408889634
F32 = jnp.float32
BF16 = jnp.bfloat16

STEPS = ((1, 0), (0, 1), (1, 1))


def dot_nt(a, b):
    return lax.dot_general(a, b, (((1,), (1,)), ((), ())), preferred_element_type=F32)


def dot(a, b):
    return jnp.dot(a, b, preferred_element_type=F32)


def kernel(
    outer_count, inner_count, heads,
    span_ref, q_hbm, k_hbm, v_hbm, do_hbm, o_hbm, lse_hbm,
    dq_hbm, dk_ref, dv_ref,
    q, do, o, own_k, own_v, lse, lse2, rdot,
    kin_a, kin_b, kin_c, vin_a, vin_b, vin_c, pin, pout, p_t, ds_t, dq_l, dq_stage,
    in_sem, ks_send, ks_recv, vs_send, vs_recv, ps_send, ps_recv, out_sem,
):
    me_o = lax.axis_index("outer")
    me_i = lax.axis_index("inner")
    pairs = heads // 2
    factor = 1.0 / math.sqrt(HD)
    kin, vin = (kin_a, kin_b, kin_c), (vin_a, vin_b, vin_c)

    loads = [
        pltpu.make_async_copy(src, dst, in_sem.at[n])
        for n, (src, dst) in enumerate(
            ((lse_hbm, lse), (k_hbm, own_k), (v_hbm, own_v), (do_hbm, do), (o_hbm, o), (q_hbm, q))
        )
    ]
    for load in loads:
        load.start()

    def ahead(step):
        return (lax.rem(me_o + step[0], outer_count), lax.rem(me_i + step[1], inner_count))

    def behind(step):
        return (
            lax.rem(me_o + outer_count - step[0], outer_count),
            lax.rem(me_i + inner_count - step[1], inner_count),
        )

    barrier = pltpu.get_barrier_semaphore()
    for step in STEPS:
        pl.semaphore_signal(barrier, inc=1, device_id=ahead(step), device_id_type=MESH)
        pl.semaphore_signal(barrier, inc=1, device_id=behind(step), device_id_type=MESH)
    pl.semaphore_wait(barrier, 2 * len(STEPS))

    k_copies, v_copies = {}, {}

    def send_block(j, k_src, v_src, to):
        for table, src, dst, ssem, rsem in (
            (k_copies, k_src, kin, ks_send, ks_recv), (v_copies, v_src, vin, vs_send, vs_recv)
        ):
            table[j] = pltpu.make_async_remote_copy(
                src_ref=src, dst_ref=dst[j], send_sem=ssem.at[j], recv_sem=rsem.at[j],
                device_id=ahead(to), device_id_type=MESH,
            )
            table[j].start()

    send_block(0, k_hbm, v_hbm, STEPS[0])
    send_block(1, k_hbm, v_hbm, STEPS[1])

    def cols(h):
        return slice(h * HD, (h + 1) * HD)

    def pair_rows(ref, half, p):
        return jnp.concatenate([ref[half, :, cols(2 * p)], ref[half, :, cols(2 * p + 1)]], axis=0)

    def all_rows(ref, half):
        return jnp.concatenate([ref[half, :, cols(h)] for h in range(heads)], axis=0)

    def pair_lanes(ref, half, p):
        return jnp.concatenate(
            [ref[half, 2 * p : 2 * p + 1, :], ref[half, 2 * p + 1 : 2 * p + 2, :]], axis=1
        )

    for load in loads[:5]:
        load.wait()
    for s in range(2):
        lse2[s] = lse[:, s * HD : (s + 1) * HD] * LOG2E
    ones = jnp.ones((16, 2 * HD), BF16)
    for s in range(2):
        for p in range(pairs):
            terms = []
            for h in (2 * p, 2 * p + 1):
                prod = do[s, :, cols(h)].astype(F32) * o[s, :, cols(h)].astype(F32)
                high = prod.astype(BF16)
                low = (prod - high.astype(F32)).astype(BF16)
                terms.append(jnp.concatenate([high, low], axis=1))
            sums = dot_nt(ones, jnp.concatenate(terms, axis=0))
            rdot[s, 2 * p : 2 * p + 1, :] = sums[0:1, :HD]
            rdot[s, 2 * p + 1 : 2 * p + 2, :] = sums[0:1, HD:]
    loads[5].wait()

    scale2 = factor * LOG2E

    def weights(keys, values, half, p, mask):
        scores = dot_nt(keys, pair_rows(q, half, p))
        dprobs = dot_nt(values, pair_rows(do, half, p))
        probs = jnp.exp2(scores * scale2 - pair_lanes(lse2, half, p))
        if mask is not None:
            probs = jnp.where(mask, probs, 0.0)
        dscores = probs * (dprobs - pair_lanes(rdot, half, p))
        return probs.astype(BF16), dscores.astype(BF16)

    k_rows = lax.broadcasted_iota(jnp.int32, (HD, 2 * HD), 0)
    q_lanes = lax.broadcasted_iota(jnp.int32, (HD, 2 * HD), 1) % HD
    triangle = k_rows <= q_lanes
    lo_k, hi_k = own_k[0], own_k[1]
    lo_v, hi_v = own_v[0], own_v[1]
    for p in range(pairs):
        lanes = slice(2 * p * HD, (2 * p + 2) * HD)
        for row, keys, values, half, mask in (
            (0, lo_k, lo_v, 0, triangle), (1, lo_k, lo_v, 1, None), (2, hi_k, hi_v, 1, triangle)
        ):
            probs, dscores = weights(keys, values, half, p, mask)
            p_t[row * HD : (row + 1) * HD, lanes] = probs
            ds_t[row * HD : (row + 1) * HD, lanes] = dscores
    k_copies[0].wait_recv()
    v_copies[0].wait_recv()
    send_block(2, kin[0], vin[0], STEPS[1])

    for out, lhs, rhs in ((dv_ref, p_t, do), (dk_ref, ds_t, q)):
        late = dot(lhs[HD : 3 * HD, :], all_rows(rhs, 1))
        out[0] = late[:HD] + dot(lhs[:HD, :], all_rows(rhs, 0))
        out[1] = late[HD:]

    zero = jnp.zeros((HD, HD), BF16)
    dq_l[0:HD, 0:HD] = zero
    dq_l[HD:, 0:HD] = lo_k.T
    dq_l[0:HD, HD : 2 * HD] = lo_k.T
    dq_l[0:HD, 2 * HD : 3 * HD] = hi_k.T
    dq_l[HD:, HD : 2 * HD] = zero
    dq_l[HD:, 2 * HD : 3 * HD] = zero

    me_span = span_ref[0, me_o * inner_count + me_i]
    p_copies = []
    for j, step in enumerate(STEPS):
        src_o, src_i = behind(step)
        src_span = span_ref[0, src_o * inner_count + src_i]
        early = src_span < me_span
        half = jnp.where(early, 0, 1)
        if j > 0:
            k_copies[j].wait_recv()
            v_copies[j].wait_recv()
        lo_k, sel_k = kin[j][0], kin[j][half]
        lo_v, sel_v = vin[j][0], vin[j][half]
        base = (3 + 2 * j) * HD
        for p in range(pairs):
            lanes = slice(2 * p * HD, (2 * p + 2) * HD)
            for row, keys, values, side in ((0, lo_k, lo_v, 1), (1, sel_k, sel_v, half)):
                probs, dscores = weights(keys, values, side, p, None)
                p_t[row * HD : (row + 1) * HD, lanes] = probs
                ds_t[base + row * HD : base + (row + 1) * HD, lanes] = dscores
        is_early = jnp.full((HD, HD), src_span, jnp.int32) < me_span
        for n, (lhs, at, rhs) in enumerate(((ds_t, base, q), (p_t, 0, do))):
            on_lo = dot(lhs[at : at + HD, :], all_rows(rhs, 1))
            on_sel = dot(lhs[at + HD : at + 2 * HD, :], all_rows(rhs, half))
            pout[j, 2 * n] = (on_lo + jnp.where(is_early, on_sel, 0.0)).astype(BF16)
            pout[j, 2 * n + 1] = jnp.where(is_early, 0.0, on_sel).astype(BF16)
        copy = pltpu.make_async_remote_copy(
            src_ref=pout.at[j], dst_ref=pin.at[j], send_sem=ps_send.at[j], recv_sem=ps_recv.at[j],
            device_id=behind(step), device_id_type=MESH,
        )
        copy.start()
        p_copies.append(copy)
        sel_t = sel_k.astype(F32).T
        dq_l[0:HD, base : base + HD] = lo_k.T
        dq_l[0:HD, base + HD : base + 2 * HD] = jnp.where(is_early, 0.0, sel_t).astype(BF16)
        dq_l[HD:, base : base + HD] = zero
        dq_l[HD:, base + HD : base + 2 * HD] = jnp.where(is_early, sel_t, 0.0).astype(BF16)

    stores = []
    for p in range(pairs):
        lanes = slice(2 * p * HD, (2 * p + 2) * HD)
        grads = dot(dq_l[...], ds_t[:, lanes]) * factor
        for s in range(2):
            for n in range(2):
                tile = grads[(1 - s) * HD : (2 - s) * HD, n * HD : (n + 1) * HD]
                dq_stage[s, :, cols(2 * p + n)] = tile.T.astype(BF16)
        store = pltpu.make_async_copy(
            dq_stage.at[:, :, lanes], dq_hbm.at[:, :, lanes], out_sem.at[p]
        )
        store.start()
        stores.append(store)

    for j in range(len(STEPS)):
        p_copies[j].wait_recv()
    for s in range(2):
        dk_ref[s] = (dk_ref[s] + sum(pin[j, s].astype(F32) for j in range(len(STEPS)))) * factor
        dv_ref[s] = dv_ref[s] + sum(pin[j, 2 + s].astype(F32) for j in range(len(STEPS)))
    for store in stores:
        store.wait()
    for j in range(len(STEPS)):
        k_copies[j].wait_send()
        v_copies[j].wait_send()
        p_copies[j].wait_send()


def place(dq, dk, dv, dq_out, dk_out, dv_out, dq_v, dk_v, dv_v, sem_in, sem_out):
    rows = dq.shape[1] // 2
    pieces = [
        tuple(ref.at[s, pl.ds(r * rows, rows), :] for ref in (dq, dq_v, dq_out))
        for s in range(2)
        for r in range(2)
    ] + [(dk, dk_v, dk_out), (dv, dv_v, dv_out)]
    loads = [pltpu.make_async_copy(src, mid, sem_in.at[n]) for n, (src, mid, _) in enumerate(pieces)]
    stores = [pltpu.make_async_copy(mid, dst, sem_out.at[n]) for n, (_, mid, dst) in enumerate(pieces)]
    for load in loads:
        load.start()
    for load, store in zip(loads, stores):
        load.wait()
        store.start()
    for store in stores:
        store.wait()


def per_device(outer_count, inner_count, queries, key_rows, value_rows, out_grad, outputs, log_sum, span_table):
    heads = log_sum.shape[0]
    rows, width = queries.shape
    half = rows // 2
    steps = len(STEPS)
    any_spec = pl.BlockSpec(memory_space=pl.ANY)
    vmem = pl.BlockSpec(memory_space=pltpu.VMEM)
    smem = pl.BlockSpec(memory_space=pltpu.SMEM)
    wide = (2, half, width)
    narrow = (2, half, HD)
    dma = pltpu.SemaphoreType.DMA
    dq, dk, dv = pl.pallas_call(
        functools.partial(kernel, outer_count, inner_count, heads),
        out_shape=(
            jax.ShapeDtypeStruct(wide, BF16),
            jax.ShapeDtypeStruct(narrow, F32),
            jax.ShapeDtypeStruct(narrow, F32),
        ),
        in_specs=[smem] + [any_spec] * 6,
        out_specs=(any_spec, vmem, vmem),
        scratch_shapes=[
            pltpu.VMEM(wide, BF16), pltpu.VMEM(wide, BF16), pltpu.VMEM(wide, BF16),
            pltpu.VMEM(narrow, BF16), pltpu.VMEM(narrow, BF16),
            pltpu.VMEM((heads, rows), F32), pltpu.VMEM((2, heads, half), F32), pltpu.VMEM((2, heads, half), F32),
            *[pltpu.VMEM(narrow, BF16) for _ in range(2 * steps)],
            pltpu.VMEM((steps, 4, half, HD), BF16), pltpu.VMEM((steps, 4, half, HD), BF16),
            pltpu.VMEM((3 * half, width), BF16),
            pltpu.VMEM(((3 + 2 * steps) * half, width), BF16),
            pltpu.VMEM((2 * HD, (3 + 2 * steps) * half), BF16),
            pltpu.VMEM(wide, BF16),
            dma((6,)), dma((steps,)), dma((steps,)), dma((steps,)), dma((steps,)),
            dma((steps,)), dma((steps,)), dma((heads // 2,)),
        ],
        compiler_params=pltpu.CompilerParams(
            collective_id=0, has_side_effects=True, vmem_limit_bytes=60 * 1024 * 1024
        ),
        cost_estimate=pl.CostEstimate(
            flops=2 * 5 * 9 * heads * half * half * HD, bytes_accessed=4 * rows * width * 2,
            transcendentals=9 * heads * half * half,
        ),
    )(
        span_table.T, queries.reshape(wide), key_rows.reshape(narrow), value_rows.reshape(narrow),
        out_grad.reshape(wide), outputs.reshape(wide), log_sum,
    )
    dq, dk, dv = pl.pallas_call(
        place,
        out_shape=(
            jax.ShapeDtypeStruct(wide, BF16),
            jax.ShapeDtypeStruct(narrow, F32),
            jax.ShapeDtypeStruct(narrow, F32),
        ),
        in_specs=[any_spec] * 3,
        out_specs=[any_spec] * 3,
        scratch_shapes=[
            pltpu.VMEM(wide, BF16), pltpu.VMEM(narrow, F32), pltpu.VMEM(narrow, F32), dma((6,)), dma((6,))
        ],
        compiler_params=pltpu.CompilerParams(vmem_limit_bytes=60 * 1024 * 1024),
    )(dq, dk, dv)
    return dq.reshape(rows, width), dk.reshape(rows, HD), dv.reshape(rows, HD)


def solution(mesh):
    rows = P(("outer", "inner"), None)
    return jax.shard_map(
        functools.partial(per_device, mesh.shape["outer"], mesh.shape["inner"]),
        mesh=mesh,
        in_specs=(rows, rows, rows, rows, rows, P(None, ("outer", "inner")), P()),
        out_specs=(rows, rows, rows),
        check_vma=False,
    )
```

```python
import functools
import math

import jax
import jax.numpy as jnp
from jax import lax
from jax.experimental import pallas as pl
from jax.experimental.pallas import tpu as pltpu
from jax.sharding import PartitionSpec as P

MESH = pl.DeviceIdType.MESH
HD = 128
LOG2E = 1.4426950408889634
F32 = jnp.float32
BF16 = jnp.bfloat16

STEPS = ((1, 0), (0, 1), (1, 1))


def dot_nt(a, b):
    return lax.dot_general(a, b, (((1,), (1,)), ((), ())), preferred_element_type=F32)


def dot(a, b):
    return jnp.dot(a, b, preferred_element_type=F32)


def kernel(
    outer_count, inner_count, heads,
    span_ref, q_hbm, k_hbm, v_hbm, do_hbm, o_hbm, lse_hbm,
    dq_hbm, own_hbm, pin,
    q, do, o, own_k, own_v, lse, lse2, rdot,
    kin_a, kin_b, kin_c, vin_a, vin_b, vin_c, pout, own, p_own, p_t, ds_t, dq_l, dq_stage,
    in_sem, ks_send, ks_recv, vs_send, vs_recv, ps_send, ps_recv, out_sem,
):
    me_o = lax.axis_index("outer")
    me_i = lax.axis_index("inner")
    pairs = heads // 2
    factor = 1.0 / math.sqrt(HD)
    kin, vin = (kin_a, kin_b, kin_c), (vin_a, vin_b, vin_c)

    loads = [
        pltpu.make_async_copy(src, dst, in_sem.at[n])
        for n, (src, dst) in enumerate(
            ((lse_hbm, lse), (k_hbm, own_k), (v_hbm, own_v), (do_hbm, do), (o_hbm, o), (q_hbm, q))
        )
    ]
    for load in loads:
        load.start()

    def ahead(step):
        return (lax.rem(me_o + step[0], outer_count), lax.rem(me_i + step[1], inner_count))

    def behind(step):
        return (
            lax.rem(me_o + outer_count - step[0], outer_count),
            lax.rem(me_i + inner_count - step[1], inner_count),
        )

    barrier = pltpu.get_barrier_semaphore()
    for step in STEPS:
        pl.semaphore_signal(barrier, inc=1, device_id=ahead(step), device_id_type=MESH)
        pl.semaphore_signal(barrier, inc=1, device_id=behind(step), device_id_type=MESH)
    pl.semaphore_wait(barrier, 2 * len(STEPS))

    k_copies, v_copies = {}, {}

    def send(j, table, src, dst, ssem, rsem):
        to = STEPS[min(j, 1)]
        table[j] = pltpu.make_async_remote_copy(
            src_ref=src, dst_ref=dst[j], send_sem=ssem.at[j], recv_sem=rsem.at[j],
            device_id=ahead(to), device_id_type=MESH,
        )
        table[j].start()

    for j in range(2):
        send(j, k_copies, k_hbm, kin, ks_send, ks_recv)
        send(j, v_copies, v_hbm, vin, vs_send, vs_recv)

    def cols(h):
        return slice(h * HD, (h + 1) * HD)

    def pair_rows(ref, half, p):
        return jnp.concatenate([ref[half, :, cols(2 * p)], ref[half, :, cols(2 * p + 1)]], axis=0)

    def all_rows(ref, half):
        return jnp.concatenate([ref[half, :, cols(h)] for h in range(heads)], axis=0)

    def pair_lanes(ref, half, p):
        return jnp.concatenate(
            [ref[half, 2 * p : 2 * p + 1, :], ref[half, 2 * p + 1 : 2 * p + 2, :]], axis=1
        )

    for load in loads[:5]:
        load.wait()
    for s in range(2):
        lse2[s] = lse[:, s * HD : (s + 1) * HD] * LOG2E
    ones = jnp.ones((16, 2 * HD), BF16)
    for s in range(2):
        for p in range(pairs):
            terms = []
            for h in (2 * p, 2 * p + 1):
                prod = do[s, :, cols(h)].astype(F32) * o[s, :, cols(h)].astype(F32)
                high = prod.astype(BF16)
                low = (prod - high.astype(F32)).astype(BF16)
                terms.append(jnp.concatenate([high, low], axis=1))
            sums = dot_nt(ones, jnp.concatenate(terms, axis=0))
            rdot[s, 2 * p : 2 * p + 1, :] = sums[0:1, :HD]
            rdot[s, 2 * p + 1 : 2 * p + 2, :] = sums[0:1, HD:]
    loads[5].wait()

    scale2 = factor * LOG2E

    def weights(keys, values, half, p, mask):
        scores = dot_nt(keys, pair_rows(q, half, p))
        dprobs = dot_nt(values, pair_rows(do, half, p))
        probs = jnp.exp2(scores * scale2 - pair_lanes(lse2, half, p))
        if mask is not None:
            probs = jnp.where(mask, probs, 0.0)
        dscores = probs * (dprobs - pair_lanes(rdot, half, p))
        return probs.astype(BF16), dscores.astype(BF16)

    k_rows = lax.broadcasted_iota(jnp.int32, (HD, 2 * HD), 0)
    q_lanes = lax.broadcasted_iota(jnp.int32, (HD, 2 * HD), 1) % HD
    triangle = k_rows <= q_lanes
    lo_k, hi_k = own_k[0], own_k[1]
    lo_v, hi_v = own_v[0], own_v[1]
    for p in range(pairs):
        lanes = slice(2 * p * HD, (2 * p + 2) * HD)
        for row, keys, values, half, mask in (
            (0, lo_k, lo_v, 0, triangle), (1, lo_k, lo_v, 1, None), (2, hi_k, hi_v, 1, triangle)
        ):
            probs, dscores = weights(keys, values, half, p, mask)
            p_own[row * HD : (row + 1) * HD, lanes] = probs
            ds_t[row * HD : (row + 1) * HD, lanes] = dscores
        if p == pairs // 4:
            k_copies[0].wait_recv()
            send(2, k_copies, kin[0], kin, ks_send, ks_recv)
        if p == pairs // 2:
            v_copies[0].wait_recv()
            send(2, v_copies, vin[0], vin, vs_send, vs_recv)

    zero = jnp.zeros((HD, HD), BF16)
    dq_l[0:HD, 0:HD] = zero
    dq_l[HD:, 0:HD] = lo_k.T
    dq_l[0:HD, HD : 2 * HD] = lo_k.T
    dq_l[0:HD, 2 * HD : 3 * HD] = hi_k.T
    dq_l[HD:, HD : 2 * HD] = zero
    dq_l[HD:, 2 * HD : 3 * HD] = zero

    me_span = span_ref[0, me_o * inner_count + me_i]
    p_copies = []
    for j, step in enumerate(STEPS):
        src_o, src_i = behind(step)
        src_span = span_ref[0, src_o * inner_count + src_i]
        early = src_span < me_span
        half = jnp.where(early, 0, 1)
        if j > 0:
            k_copies[j].wait_recv()
            v_copies[j].wait_recv()
        lo_k, sel_k = kin[j][0], kin[j][half]
        lo_v, sel_v = vin[j][0], vin[j][half]
        base = (3 + 2 * j) * HD
        for p in range(pairs):
            lanes = slice(2 * p * HD, (2 * p + 2) * HD)
            for row, keys, values, side in ((0, lo_k, lo_v, 1), (1, sel_k, sel_v, half)):
                probs, dscores = weights(keys, values, side, p, None)
                p_t[row * HD : (row + 1) * HD, lanes] = probs
                ds_t[base + row * HD : base + (row + 1) * HD, lanes] = dscores
        is_early = jnp.full((HD, HD), src_span, jnp.int32) < me_span
        for n, lhs, at, rhs in ((1, p_t, 0, do), (0, ds_t, base, q)):
            on_lo = dot(lhs[at : at + HD, :], all_rows(rhs, 1))
            on_sel = dot(lhs[at + HD : at + 2 * HD, :], all_rows(rhs, half))
            pout[j, 2 * n] = (on_lo + jnp.where(is_early, on_sel, 0.0)).astype(BF16)
            pout[j, 2 * n + 1] = jnp.where(is_early, 0.0, on_sel).astype(BF16)
            part = pl.ds(2 * n, 2)
            copy = pltpu.make_async_remote_copy(
                src_ref=pout.at[j, part], dst_ref=pin.at[j, part],
                send_sem=ps_send.at[2 * j + n], recv_sem=ps_recv.at[2 * j + n],
                device_id=behind(step), device_id_type=MESH,
            )
            copy.start()
            p_copies.append(copy)
        sel_t = sel_k.astype(F32).T
        dq_l[0:HD, base : base + HD] = lo_k.T
        dq_l[0:HD, base + HD : base + 2 * HD] = jnp.where(is_early, 0.0, sel_t).astype(BF16)
        dq_l[HD:, base : base + HD] = zero
        dq_l[HD:, base + HD : base + 2 * HD] = jnp.where(is_early, sel_t, 0.0).astype(BF16)

    for n, lhs, rhs in ((0, ds_t, q), (1, p_own, do)):
        late = dot(lhs[HD : 3 * HD, :], all_rows(rhs, 1))
        own[n, 0] = late[:HD] + dot(lhs[:HD, :], all_rows(rhs, 0))
        own[n, 1] = late[HD:]
    own_store = pltpu.make_async_copy(own, own_hbm, out_sem.at[pairs])
    own_store.start()

    stores = []
    for p in range(pairs):
        lanes = slice(2 * p * HD, (2 * p + 2) * HD)
        grads = dot(dq_l[...], ds_t[:, lanes]) * factor
        for s in range(2):
            for n in range(2):
                tile = grads[(1 - s) * HD : (2 - s) * HD, n * HD : (n + 1) * HD]
                dq_stage[s, :, cols(2 * p + n)] = tile.T.astype(BF16)
        store = pltpu.make_async_copy(
            dq_stage.at[:, :, lanes], dq_hbm.at[:, :, lanes], out_sem.at[p]
        )
        store.start()
        stores.append(store)

    own_store.wait()
    for store in stores:
        store.wait()
    for copy in p_copies:
        copy.wait_recv()
    for j in range(len(STEPS)):
        k_copies[j].wait_send()
        v_copies[j].wait_send()
    for copy in p_copies:
        copy.wait_send()


def place(dq, own, parts, dq_out, dk_out, dv_out, dq_v, own_v, parts_v, dk_v, dv_v, sem_in, sem_out):
    rows = dq.shape[1] // 2
    pieces = [
        tuple(ref.at[s, pl.ds(r * rows, rows), :] for ref in (dq, dq_v, dq_out))
        for s in range(2)
        for r in range(2)
    ]
    count = len(pieces)
    moves = [(own, own_v), (parts, parts_v)] + [piece[:2] for piece in pieces]
    loads = [pltpu.make_async_copy(src, mid, sem_in.at[n]) for n, (src, mid) in enumerate(moves)]
    moves = [piece[1:] for piece in pieces] + [(dk_v, dk_out), (dv_v, dv_out)]
    stores = [pltpu.make_async_copy(mid, dst, sem_out.at[n]) for n, (mid, dst) in enumerate(moves)]
    for load in loads:
        load.start()
    loads[0].wait()
    loads[1].wait()
    for n, (out, scale) in enumerate(((dk_v, 1.0 / math.sqrt(HD)), (dv_v, 1.0))):
        for s in range(2):
            total = own_v[n, s]
            for j in range(parts.shape[0]):
                total = total + parts_v[j, 2 * n + s].astype(F32)
            out[s] = total * scale
        stores[count + n].start()
    for n in range(count):
        loads[2 + n].wait()
        stores[n].start()
    for store in stores:
        store.wait()


def per_device(outer_count, inner_count, queries, key_rows, value_rows, out_grad, outputs, log_sum, span_table):
    heads = log_sum.shape[0]
    rows, width = queries.shape
    half = rows // 2
    steps = len(STEPS)
    any_spec = pl.BlockSpec(memory_space=pl.ANY)
    smem = pl.BlockSpec(memory_space=pltpu.SMEM)
    wide = (2, half, width)
    narrow = (2, half, HD)
    dma = pltpu.SemaphoreType.DMA
    dq, own, parts = pl.pallas_call(
        functools.partial(kernel, outer_count, inner_count, heads),
        out_shape=(
            jax.ShapeDtypeStruct(wide, BF16),
            jax.ShapeDtypeStruct((2,) + narrow, F32),
            jax.ShapeDtypeStruct((steps, 4, half, HD), BF16),
        ),
        in_specs=[smem] + [any_spec] * 6,
        out_specs=(any_spec,) * 3,
        scratch_shapes=[
            pltpu.VMEM(wide, BF16), pltpu.VMEM(wide, BF16), pltpu.VMEM(wide, BF16),
            pltpu.VMEM(narrow, BF16), pltpu.VMEM(narrow, BF16),
            pltpu.VMEM((heads, rows), F32), pltpu.VMEM((2, heads, half), F32), pltpu.VMEM((2, heads, half), F32),
            *[pltpu.VMEM(narrow, BF16) for _ in range(2 * steps)],
            pltpu.VMEM((steps, 4, half, HD), BF16), pltpu.VMEM((2,) + narrow, F32),
            pltpu.VMEM((3 * half, width), BF16), pltpu.VMEM((2 * half, width), BF16),
            pltpu.VMEM(((3 + 2 * steps) * half, width), BF16),
            pltpu.VMEM((2 * HD, (3 + 2 * steps) * half), BF16),
            pltpu.VMEM(wide, BF16),
            dma((6,)), dma((steps,)), dma((steps,)), dma((steps,)), dma((steps,)),
            dma((2 * steps,)), dma((2 * steps,)), dma((heads // 2 + 1,)),
        ],
        compiler_params=pltpu.CompilerParams(
            collective_id=0, has_side_effects=True, vmem_limit_bytes=60 * 1024 * 1024
        ),
        cost_estimate=pl.CostEstimate(
            flops=2 * 5 * 9 * heads * half * half * HD, bytes_accessed=4 * rows * width * 2,
            transcendentals=9 * heads * half * half,
        ),
    )(
        span_table.T, queries.reshape(wide), key_rows.reshape(narrow), value_rows.reshape(narrow),
        out_grad.reshape(wide), outputs.reshape(wide), log_sum,
    )
    dq, dk, dv = pl.pallas_call(
        place,
        out_shape=(
            jax.ShapeDtypeStruct(wide, BF16),
            jax.ShapeDtypeStruct(narrow, F32),
            jax.ShapeDtypeStruct(narrow, F32),
        ),
        in_specs=[any_spec] * 3,
        out_specs=[any_spec] * 3,
        scratch_shapes=[
            pltpu.VMEM(wide, BF16), pltpu.VMEM((2,) + narrow, F32), pltpu.VMEM((steps, 4, half, HD), BF16),
            pltpu.VMEM(narrow, F32), pltpu.VMEM(narrow, F32), dma((6,)), dma((6,)),
        ],
        compiler_params=pltpu.CompilerParams(vmem_limit_bytes=60 * 1024 * 1024),
    )(dq, own, parts)
    return dq.reshape(rows, width), dk.reshape(rows, HD), dv.reshape(rows, HD)


def solution(mesh):
    rows = P(("outer", "inner"), None)
    return jax.shard_map(
        functools.partial(per_device, mesh.shape["outer"], mesh.shape["inner"]),
        mesh=mesh,
        in_specs=(rows, rows, rows, rows, rows, P(None, ("outer", "inner")), P()),
        out_specs=(rows, rows, rows),
        check_vma=False,
    )
```

```python
import functools
import math

import jax
import jax.numpy as jnp
from jax import lax
from jax.experimental import pallas as pl
from jax.experimental.pallas import tpu as pltpu
from jax.sharding import PartitionSpec as P

MESH = pl.DeviceIdType.MESH
HD = 128
LOG2E = 1.4426950408889634
F32 = jnp.float32
BF16 = jnp.bfloat16

STEPS = ((1, 0), (0, 1), (1, 1))


def dot_nt(a, b):
    return lax.dot_general(a, b, (((1,), (1,)), ((), ())), preferred_element_type=F32)


def dot(a, b):
    return jnp.dot(a, b, preferred_element_type=F32)


def kernel(
    outer_count, inner_count, heads,
    span_ref, q_hbm, k_hbm, v_hbm, do_hbm, o_hbm, lse_hbm,
    dq_hbm, own_hbm, pin,
    q, do, o, own_k, own_v, lse, lse2, rdot,
    kin_a, kin_b, kin_c, vin_a, vin_b, vin_c, pout, own, p_own, p_t, ds_t, dq_l, dq_stage,
    in_sem, ks_send, ks_recv, vs_send, vs_recv, ps_send, ps_recv, out_sem,
):
    me_o = lax.axis_index("outer")
    me_i = lax.axis_index("inner")
    pairs = heads // 2
    factor = 1.0 / math.sqrt(HD)
    kin, vin = (kin_a, kin_b, kin_c), (vin_a, vin_b, vin_c)

    loads = [
        pltpu.make_async_copy(src, dst, in_sem.at[n])
        for n, (src, dst) in enumerate(
            ((lse_hbm, lse), (k_hbm, own_k), (v_hbm, own_v), (do_hbm, do), (o_hbm, o), (q_hbm, q))
        )
    ]
    for load in loads:
        load.start()

    def ahead(step):
        return (lax.rem(me_o + step[0], outer_count), lax.rem(me_i + step[1], inner_count))

    def behind(step):
        return (
            lax.rem(me_o + outer_count - step[0], outer_count),
            lax.rem(me_i + inner_count - step[1], inner_count),
        )

    barrier = pltpu.get_barrier_semaphore()
    for step in STEPS:
        pl.semaphore_signal(barrier, inc=1, device_id=ahead(step), device_id_type=MESH)
        pl.semaphore_signal(barrier, inc=1, device_id=behind(step), device_id_type=MESH)
    pl.semaphore_wait(barrier, 2 * len(STEPS))

    k_copies, v_copies = {}, {}

    def send(j, table, src, dst, ssem, rsem):
        to = STEPS[min(j, 1)]
        table[j] = pltpu.make_async_remote_copy(
            src_ref=src, dst_ref=dst[j], send_sem=ssem.at[j], recv_sem=rsem.at[j],
            device_id=ahead(to), device_id_type=MESH,
        )

    for j in range(3):
        send(j, k_copies, kin[0] if j == 2 else k_hbm, kin, ks_send, ks_recv)
        send(j, v_copies, vin[0] if j == 2 else v_hbm, vin, vs_send, vs_recv)
    for j in range(2):
        k_copies[j].start()
        v_copies[j].start()

    def cols(h):
        return slice(h * HD, (h + 1) * HD)

    def head_lanes(h):
        return pl.ds(pl.multiple_of(h * HD, HD), HD)

    def two_lanes(p):
        return pl.ds(pl.multiple_of(p * 2 * HD, 2 * HD), 2 * HD)

    def pair_rows(ref, half, p):
        return jnp.concatenate(
            [ref[half, :, head_lanes(2 * p)], ref[half, :, head_lanes(2 * p + 1)]], axis=0
        )

    def over_pairs(body):
        def turn(n, carry):
            body(2 * n)
            body(2 * n + 1)
            return carry

        lax.fori_loop(0, pairs // 2, turn, 0)

    def all_rows(ref, half):
        return jnp.concatenate([ref[half, :, cols(h)] for h in range(heads)], axis=0)

    def pair_lanes(ref, half, p):
        return jnp.concatenate(
            [ref[half, pl.ds(2 * p, 1), :], ref[half, pl.ds(2 * p + 1, 1), :]], axis=1
        )

    for load in loads[:5]:
        load.wait()
    for s in range(2):
        lse2[s] = lse[:, s * HD : (s + 1) * HD] * LOG2E
    ones = jnp.ones((16, 2 * HD), BF16)

    def row_dots(p):
        for s in range(2):
            terms = []
            for h in (2 * p, 2 * p + 1):
                prod = do[s, :, head_lanes(h)].astype(F32) * o[s, :, head_lanes(h)].astype(F32)
                high = prod.astype(BF16)
                low = (prod - high.astype(F32)).astype(BF16)
                terms.append(jnp.concatenate([high, low], axis=1))
            sums = dot_nt(ones, jnp.concatenate(terms, axis=0))
            rdot[s, pl.ds(2 * p, 1), :] = sums[0:1, :HD]
            rdot[s, pl.ds(2 * p + 1, 1), :] = sums[0:1, HD:]

    over_pairs(row_dots)
    loads[5].wait()

    scale2 = factor * LOG2E

    def weights(keys, values, half, p, mask):
        scores = dot_nt(keys, pair_rows(q, half, p))
        dprobs = dot_nt(values, pair_rows(do, half, p))
        probs = jnp.exp2(scores * scale2 - pair_lanes(lse2, half, p))
        if mask is not None:
            probs = jnp.where(mask, probs, 0.0)
        dscores = probs * (dprobs - pair_lanes(rdot, half, p))
        return probs.astype(BF16), dscores.astype(BF16)

    k_rows = lax.broadcasted_iota(jnp.int32, (HD, 2 * HD), 0)
    q_lanes = lax.broadcasted_iota(jnp.int32, (HD, 2 * HD), 1) % HD
    triangle = k_rows <= q_lanes
    lo_k, hi_k = own_k[0], own_k[1]
    lo_v, hi_v = own_v[0], own_v[1]

    def own_pair(p):
        lanes = two_lanes(p)
        for row, keys, values, half, mask in (
            (0, lo_k, lo_v, 0, triangle), (1, lo_k, lo_v, 1, None), (2, hi_k, hi_v, 1, triangle)
        ):
            probs, dscores = weights(keys, values, half, p, mask)
            p_own[row * HD : (row + 1) * HD, lanes] = probs
            ds_t[row * HD : (row + 1) * HD, lanes] = dscores

    def own_turn(n, carry):
        @pl.when(n == 1)
        def _():
            k_copies[0].wait_recv()
            k_copies[2].start()

        @pl.when(n == 2)
        def _():
            v_copies[0].wait_recv()
            v_copies[2].start()

        own_pair(2 * n)
        own_pair(2 * n + 1)
        return carry

    lax.fori_loop(0, pairs // 2, own_turn, 0)

    zero = jnp.zeros((HD, HD), BF16)
    dq_l[0:HD, 0:HD] = zero
    dq_l[HD:, 0:HD] = lo_k.T
    dq_l[0:HD, HD : 2 * HD] = lo_k.T
    dq_l[0:HD, 2 * HD : 3 * HD] = hi_k.T
    dq_l[HD:, HD : 2 * HD] = zero
    dq_l[HD:, 2 * HD : 3 * HD] = zero

    me_span = span_ref[0, me_o * inner_count + me_i]
    p_copies = []
    for j, step in enumerate(STEPS):
        src_o, src_i = behind(step)
        src_span = span_ref[0, src_o * inner_count + src_i]
        early = src_span < me_span
        half = jnp.where(early, 0, 1)
        if j > 0:
            k_copies[j].wait_recv()
            v_copies[j].wait_recv()
        lo_k, sel_k = kin[j][0], kin[j][half]
        lo_v, sel_v = vin[j][0], vin[j][half]
        base = (3 + 2 * j) * HD

        def other_pair(p):
            lanes = two_lanes(p)
            for row, keys, values, side in ((0, lo_k, lo_v, 1), (1, sel_k, sel_v, half)):
                probs, dscores = weights(keys, values, side, p, None)
                p_t[row * HD : (row + 1) * HD, lanes] = probs
                ds_t[base + row * HD : base + (row + 1) * HD, lanes] = dscores

        over_pairs(other_pair)
        is_early = jnp.full((HD, HD), src_span, jnp.int32) < me_span
        for n, lhs, at, rhs in ((1, p_t, 0, do), (0, ds_t, base, q)):
            on_lo = dot(lhs[at : at + HD, :], all_rows(rhs, 1))
            on_sel = dot(lhs[at + HD : at + 2 * HD, :], all_rows(rhs, half))
            pout[j, 2 * n] = (on_lo + jnp.where(is_early, on_sel, 0.0)).astype(BF16)
            pout[j, 2 * n + 1] = jnp.where(is_early, 0.0, on_sel).astype(BF16)
            part = pl.ds(2 * n, 2)
            copy = pltpu.make_async_remote_copy(
                src_ref=pout.at[j, part], dst_ref=pin.at[j, part],
                send_sem=ps_send.at[2 * j + n], recv_sem=ps_recv.at[2 * j + n],
                device_id=behind(step), device_id_type=MESH,
            )
            copy.start()
            p_copies.append(copy)
        sel_t = sel_k.astype(F32).T
        dq_l[0:HD, base : base + HD] = lo_k.T
        dq_l[0:HD, base + HD : base + 2 * HD] = jnp.where(is_early, 0.0, sel_t).astype(BF16)
        dq_l[HD:, base : base + HD] = zero
        dq_l[HD:, base + HD : base + 2 * HD] = jnp.where(is_early, sel_t, 0.0).astype(BF16)

    for n, lhs, rhs in ((0, ds_t, q), (1, p_own, do)):
        late = dot(lhs[HD : 3 * HD, :], all_rows(rhs, 1))
        own[n, 0] = late[:HD] + dot(lhs[:HD, :], all_rows(rhs, 0))
        own[n, 1] = late[HD:]
    own_store = pltpu.make_async_copy(own, own_hbm, out_sem.at[pairs])
    own_store.start()

    def query_store(p):
        return pltpu.make_async_copy(
            dq_stage.at[:, :, two_lanes(p)], dq_hbm.at[:, :, two_lanes(p)], out_sem.at[p]
        )

    def query_pair(p):
        grads = dot(dq_l[...], ds_t[:, two_lanes(p)]) * factor
        for s in range(2):
            for n in range(2):
                tile = grads[(1 - s) * HD : (2 - s) * HD, n * HD : (n + 1) * HD]
                dq_stage[s, :, head_lanes(2 * p + n)] = tile.T.astype(BF16)
        query_store(p).start()

    over_pairs(query_pair)
    stores = [query_store(p) for p in range(pairs)]
    own_store.wait()
    for store in stores:
        store.wait()
    for copy in p_copies:
        copy.wait_recv()
    for j in range(len(STEPS)):
        k_copies[j].wait_send()
        v_copies[j].wait_send()
    for copy in p_copies:
        copy.wait_send()


def place(dq, own, parts, dq_out, dk_out, dv_out, dq_v, own_v, parts_v, dk_v, dv_v, sem_in, sem_out):
    rows = dq.shape[1] // 2
    pieces = [
        tuple(ref.at[s, pl.ds(r * rows, rows), :] for ref in (dq, dq_v, dq_out))
        for s in range(2)
        for r in range(2)
    ]
    count = len(pieces)
    moves = [(own, own_v), (parts, parts_v)] + [piece[:2] for piece in pieces]
    loads = [pltpu.make_async_copy(src, mid, sem_in.at[n]) for n, (src, mid) in enumerate(moves)]
    moves = [piece[1:] for piece in pieces] + [(dk_v, dk_out), (dv_v, dv_out)]
    stores = [pltpu.make_async_copy(mid, dst, sem_out.at[n]) for n, (mid, dst) in enumerate(moves)]
    for load in loads:
        load.start()
    loads[0].wait()
    loads[1].wait()
    for n, (out, scale) in enumerate(((dk_v, 1.0 / math.sqrt(HD)), (dv_v, 1.0))):
        for s in range(2):
            total = own_v[n, s]
            for j in range(parts.shape[0]):
                total = total + parts_v[j, 2 * n + s].astype(F32)
            out[s] = total * scale
        stores[count + n].start()
    for n in range(count):
        loads[2 + n].wait()
        stores[n].start()
    for store in stores:
        store.wait()


def per_device(outer_count, inner_count, queries, key_rows, value_rows, out_grad, outputs, log_sum, span_table):
    heads = log_sum.shape[0]
    rows, width = queries.shape
    half = rows // 2
    steps = len(STEPS)
    any_spec = pl.BlockSpec(memory_space=pl.ANY)
    smem = pl.BlockSpec(memory_space=pltpu.SMEM)
    wide = (2, half, width)
    narrow = (2, half, HD)
    dma = pltpu.SemaphoreType.DMA
    dq, own, parts = pl.pallas_call(
        functools.partial(kernel, outer_count, inner_count, heads),
        out_shape=(
            jax.ShapeDtypeStruct(wide, BF16),
            jax.ShapeDtypeStruct((2,) + narrow, F32),
            jax.ShapeDtypeStruct((steps, 4, half, HD), BF16),
        ),
        in_specs=[smem] + [any_spec] * 6,
        out_specs=(any_spec,) * 3,
        scratch_shapes=[
            pltpu.VMEM(wide, BF16), pltpu.VMEM(wide, BF16), pltpu.VMEM(wide, BF16),
            pltpu.VMEM(narrow, BF16), pltpu.VMEM(narrow, BF16),
            pltpu.VMEM((heads, rows), F32), pltpu.VMEM((2, heads, half), F32), pltpu.VMEM((2, heads, half), F32),
            *[pltpu.VMEM(narrow, BF16) for _ in range(2 * steps)],
            pltpu.VMEM((steps, 4, half, HD), BF16), pltpu.VMEM((2,) + narrow, F32),
            pltpu.VMEM((3 * half, width), BF16), pltpu.VMEM((2 * half, width), BF16),
            pltpu.VMEM(((3 + 2 * steps) * half, width), BF16),
            pltpu.VMEM((2 * HD, (3 + 2 * steps) * half), BF16),
            pltpu.VMEM(wide, BF16),
            dma((6,)), dma((steps,)), dma((steps,)), dma((steps,)), dma((steps,)),
            dma((2 * steps,)), dma((2 * steps,)), dma((heads // 2 + 1,)),
        ],
        compiler_params=pltpu.CompilerParams(
            collective_id=0, has_side_effects=True, vmem_limit_bytes=60 * 1024 * 1024
        ),
        cost_estimate=pl.CostEstimate(
            flops=2 * 5 * 9 * heads * half * half * HD, bytes_accessed=4 * rows * width * 2,
            transcendentals=9 * heads * half * half,
        ),
    )(
        span_table.T, queries.reshape(wide), key_rows.reshape(narrow), value_rows.reshape(narrow),
        out_grad.reshape(wide), outputs.reshape(wide), log_sum,
    )
    dq, dk, dv = pl.pallas_call(
        place,
        out_shape=(
            jax.ShapeDtypeStruct(wide, BF16),
            jax.ShapeDtypeStruct(narrow, F32),
            jax.ShapeDtypeStruct(narrow, F32),
        ),
        in_specs=[any_spec] * 3,
        out_specs=[any_spec] * 3,
        scratch_shapes=[
            pltpu.VMEM(wide, BF16), pltpu.VMEM((2,) + narrow, F32), pltpu.VMEM((steps, 4, half, HD), BF16),
            pltpu.VMEM(narrow, F32), pltpu.VMEM(narrow, F32), dma((6,)), dma((6,)),
        ],
        compiler_params=pltpu.CompilerParams(vmem_limit_bytes=60 * 1024 * 1024),
    )(dq, own, parts)
    return dq.reshape(rows, width), dk.reshape(rows, HD), dv.reshape(rows, HD)


def solution(mesh):
    rows = P(("outer", "inner"), None)
    return jax.shard_map(
        functools.partial(per_device, mesh.shape["outer"], mesh.shape["inner"]),
        mesh=mesh,
        in_specs=(rows, rows, rows, rows, rows, P(None, ("outer", "inner")), P()),
        out_specs=(rows, rows, rows),
        check_vma=False,
    )
```

```python
import functools
import math

import jax
import jax.numpy as jnp
from jax import lax
from jax.experimental import pallas as pl
from jax.experimental.pallas import tpu as pltpu
from jax.sharding import PartitionSpec as P

MESH = pl.DeviceIdType.MESH
HD = 128
LOG2E = 1.4426950408889634
F32 = jnp.float32
BF16 = jnp.bfloat16

STEPS = ((1, 0), (0, 1), (1, 1))


def dot_nt(a, b):
    return lax.dot_general(a, b, (((1,), (1,)), ((), ())), preferred_element_type=F32)


def dot(a, b):
    return jnp.dot(a, b, preferred_element_type=F32)


def kernel(
    outer_count, inner_count, heads,
    span_ref, q_hbm, k_hbm, v_hbm, do_hbm, o_hbm, lse_hbm,
    dq_hbm, own_hbm, pin,
    q, do, o, own_k, own_v, lse, lse2, rdot,
    kin_a, kin_b, kin_c, vin_a, vin_b, vin_c, pout, own, p_own, p_t, ds_t, dq_l, dq_stage,
    in_sem, ks_send, ks_recv, vs_send, vs_recv, ps_send, ps_recv, out_sem,
):
    me_o = lax.axis_index("outer")
    me_i = lax.axis_index("inner")
    pairs = heads // 2
    factor = 1.0 / math.sqrt(HD)
    kin, vin = (kin_a, kin_b, kin_c), (vin_a, vin_b, vin_c)

    loads = [
        pltpu.make_async_copy(src, dst, in_sem.at[n])
        for n, (src, dst) in enumerate(
            ((lse_hbm, lse), (k_hbm, own_k), (v_hbm, own_v), (do_hbm, do), (o_hbm, o), (q_hbm, q))
        )
    ]
    for load in loads:
        load.start()

    def ahead(step):
        return (lax.rem(me_o + step[0], outer_count), lax.rem(me_i + step[1], inner_count))

    def behind(step):
        return (
            lax.rem(me_o + outer_count - step[0], outer_count),
            lax.rem(me_i + inner_count - step[1], inner_count),
        )

    barrier = pltpu.get_barrier_semaphore()
    for step in STEPS:
        pl.semaphore_signal(barrier, inc=1, device_id=ahead(step), device_id_type=MESH)
        pl.semaphore_signal(barrier, inc=1, device_id=behind(step), device_id_type=MESH)
    pl.semaphore_wait(barrier, 2 * len(STEPS))

    k_copies, v_copies = {}, {}

    def send(j, table, src, dst, ssem, rsem):
        to = STEPS[min(j, 1)]
        table[j] = pltpu.make_async_remote_copy(
            src_ref=src, dst_ref=dst[j], send_sem=ssem.at[j], recv_sem=rsem.at[j],
            device_id=ahead(to), device_id_type=MESH,
        )
        table[j].start()

    for j in range(2):
        send(j, k_copies, k_hbm, kin, ks_send, ks_recv)
        send(j, v_copies, v_hbm, vin, vs_send, vs_recv)

    def cols(h):
        return slice(h * HD, (h + 1) * HD)

    def pair_rows(ref, half, p):
        return jnp.concatenate([ref[half, :, cols(2 * p)], ref[half, :, cols(2 * p + 1)]], axis=0)

    def all_rows(ref, half):
        return jnp.concatenate([ref[half, :, cols(h)] for h in range(heads)], axis=0)

    def pair_lanes(ref, half, p):
        return jnp.concatenate(
            [ref[half, 2 * p : 2 * p + 1, :], ref[half, 2 * p + 1 : 2 * p + 2, :]], axis=1
        )

    for load in loads[:5]:
        load.wait()
    for s in range(2):
        lse2[s] = lse[:, s * HD : (s + 1) * HD] * LOG2E
    ones = jnp.ones((16, 2 * HD), BF16)
    for s in range(2):
        for p in range(pairs):
            terms = []
            for h in (2 * p, 2 * p + 1):
                prod = do[s, :, cols(h)].astype(F32) * o[s, :, cols(h)].astype(F32)
                high = prod.astype(BF16)
                low = (prod - high.astype(F32)).astype(BF16)
                terms.append(jnp.concatenate([high, low], axis=1))
            sums = dot_nt(ones, jnp.concatenate(terms, axis=0))
            rdot[s, 2 * p : 2 * p + 1, :] = sums[0:1, :HD]
            rdot[s, 2 * p + 1 : 2 * p + 2, :] = sums[0:1, HD:]
    loads[5].wait()

    scale2 = factor * LOG2E

    def weights(keys, values, half, p, mask):
        scores = dot_nt(keys, pair_rows(q, half, p))
        dprobs = dot_nt(values, pair_rows(do, half, p))
        probs = jnp.exp2(scores * scale2 - pair_lanes(lse2, half, p))
        if mask is not None:
            probs = jnp.where(mask, probs, 0.0)
        dscores = probs * (dprobs - pair_lanes(rdot, half, p))
        return probs.astype(BF16), dscores.astype(BF16)

    k_rows = lax.broadcasted_iota(jnp.int32, (HD, 2 * HD), 0)
    q_lanes = lax.broadcasted_iota(jnp.int32, (HD, 2 * HD), 1) % HD
    triangle = k_rows <= q_lanes
    lo_k, hi_k = own_k[0], own_k[1]
    lo_v, hi_v = own_v[0], own_v[1]
    for p in range(pairs):
        lanes = slice(2 * p * HD, (2 * p + 2) * HD)
        for row, keys, values, half, mask in (
            (0, lo_k, lo_v, 0, triangle), (1, lo_k, lo_v, 1, None), (2, hi_k, hi_v, 1, triangle)
        ):
            probs, dscores = weights(keys, values, half, p, mask)
            p_own[row * HD : (row + 1) * HD, lanes] = probs
            ds_t[row * HD : (row + 1) * HD, lanes] = dscores
        if p == pairs // 4:
            k_copies[0].wait_recv()
            send(2, k_copies, kin[0], kin, ks_send, ks_recv)
        if p == pairs // 2:
            v_copies[0].wait_recv()
            send(2, v_copies, vin[0], vin, vs_send, vs_recv)

    zero = jnp.zeros((HD, HD), BF16)
    dq_l[0:HD, 0:HD] = zero
    dq_l[HD:, 0:HD] = lo_k.T
    dq_l[0:HD, HD : 2 * HD] = lo_k.T
    dq_l[0:HD, 2 * HD : 3 * HD] = hi_k.T
    dq_l[HD:, HD : 2 * HD] = zero
    dq_l[HD:, 2 * HD : 3 * HD] = zero

    me_span = span_ref[0, me_o * inner_count + me_i]
    p_copies = []
    for j in (0, 2, 1):
        step = STEPS[j]
        src_o, src_i = behind(step)
        src_span = span_ref[0, src_o * inner_count + src_i]
        early = src_span < me_span
        half = jnp.where(early, 0, 1)
        if j > 0:
            k_copies[j].wait_recv()
            v_copies[j].wait_recv()
        lo_k, sel_k = kin[j][0], kin[j][half]
        lo_v, sel_v = vin[j][0], vin[j][half]
        base = (3 + 2 * j) * HD
        for p in range(pairs):
            lanes = slice(2 * p * HD, (2 * p + 2) * HD)
            for row, keys, values, side in ((0, lo_k, lo_v, 1), (1, sel_k, sel_v, half)):
                probs, dscores = weights(keys, values, side, p, None)
                p_t[row * HD : (row + 1) * HD, lanes] = probs
                ds_t[base + row * HD : base + (row + 1) * HD, lanes] = dscores
        is_early = jnp.full((HD, HD), src_span, jnp.int32) < me_span
        for n, lhs, at, rhs in ((1, p_t, 0, do), (0, ds_t, base, q)):
            on_lo = dot(lhs[at : at + HD, :], all_rows(rhs, 1))
            on_sel = dot(lhs[at + HD : at + 2 * HD, :], all_rows(rhs, half))
            pout[j, 2 * n] = (on_lo + jnp.where(is_early, on_sel, 0.0)).astype(BF16)
            pout[j, 2 * n + 1] = jnp.where(is_early, 0.0, on_sel).astype(BF16)
            part = pl.ds(2 * n, 2)
            copy = pltpu.make_async_remote_copy(
                src_ref=pout.at[j, part], dst_ref=pin.at[j, part],
                send_sem=ps_send.at[2 * j + n], recv_sem=ps_recv.at[2 * j + n],
                device_id=behind(step), device_id_type=MESH,
            )
            copy.start()
            p_copies.append(copy)
        sel_t = sel_k.astype(F32).T
        dq_l[0:HD, base : base + HD] = lo_k.T
        dq_l[0:HD, base + HD : base + 2 * HD] = jnp.where(is_early, 0.0, sel_t).astype(BF16)
        dq_l[HD:, base : base + HD] = zero
        dq_l[HD:, base + HD : base + 2 * HD] = jnp.where(is_early, sel_t, 0.0).astype(BF16)

    for n, lhs, rhs in ((0, ds_t, q), (1, p_own, do)):
        late = dot(lhs[HD : 3 * HD, :], all_rows(rhs, 1))
        own[n, 0] = late[:HD] + dot(lhs[:HD, :], all_rows(rhs, 0))
        own[n, 1] = late[HD:]
    own_store = pltpu.make_async_copy(own, own_hbm, out_sem.at[pairs])
    own_store.start()

    stores = []
    for p in range(pairs):
        lanes = slice(2 * p * HD, (2 * p + 2) * HD)
        grads = dot(dq_l[...], ds_t[:, lanes]) * factor
        for s in range(2):
            for n in range(2):
                tile = grads[(1 - s) * HD : (2 - s) * HD, n * HD : (n + 1) * HD]
                dq_stage[s, :, cols(2 * p + n)] = tile.T.astype(BF16)
        store = pltpu.make_async_copy(
            dq_stage.at[:, :, lanes], dq_hbm.at[:, :, lanes], out_sem.at[p]
        )
        store.start()
        stores.append(store)

    own_store.wait()
    for store in stores:
        store.wait()
    for copy in p_copies:
        copy.wait_recv()
    for j in range(len(STEPS)):
        k_copies[j].wait_send()
        v_copies[j].wait_send()
    for copy in p_copies:
        copy.wait_send()


def place(dq, own, parts, dq_out, dk_out, dv_out, dq_v, own_v, parts_v, dk_v, dv_v, sem_in, sem_out):
    rows = dq.shape[1] // 2
    pieces = [
        tuple(ref.at[s, pl.ds(r * rows, rows), :] for ref in (dq, dq_v, dq_out))
        for s in range(2)
        for r in range(2)
    ]
    count = len(pieces)
    moves = [(own, own_v), (parts, parts_v)] + [piece[:2] for piece in pieces]
    loads = [pltpu.make_async_copy(src, mid, sem_in.at[n]) for n, (src, mid) in enumerate(moves)]
    moves = [piece[1:] for piece in pieces] + [(dk_v, dk_out), (dv_v, dv_out)]
    stores = [pltpu.make_async_copy(mid, dst, sem_out.at[n]) for n, (mid, dst) in enumerate(moves)]
    for load in loads:
        load.start()
    loads[0].wait()
    loads[1].wait()
    for n, (out, scale) in enumerate(((dk_v, 1.0 / math.sqrt(HD)), (dv_v, 1.0))):
        for s in range(2):
            total = own_v[n, s]
            for j in range(parts.shape[0]):
                total = total + parts_v[j, 2 * n + s].astype(F32)
            out[s] = total * scale
        stores[count + n].start()
    for n in range(count):
        loads[2 + n].wait()
        stores[n].start()
    for store in stores:
        store.wait()


def per_device(outer_count, inner_count, queries, key_rows, value_rows, out_grad, outputs, log_sum, span_table):
    heads = log_sum.shape[0]
    rows, width = queries.shape
    half = rows // 2
    steps = len(STEPS)
    any_spec = pl.BlockSpec(memory_space=pl.ANY)
    smem = pl.BlockSpec(memory_space=pltpu.SMEM)
    wide = (2, half, width)
    narrow = (2, half, HD)
    dma = pltpu.SemaphoreType.DMA
    dq, own, parts = pl.pallas_call(
        functools.partial(kernel, outer_count, inner_count, heads),
        out_shape=(
            jax.ShapeDtypeStruct(wide, BF16),
            jax.ShapeDtypeStruct((2,) + narrow, F32),
            jax.ShapeDtypeStruct((steps, 4, half, HD), BF16),
        ),
        in_specs=[smem] + [any_spec] * 6,
        out_specs=(any_spec,) * 3,
        scratch_shapes=[
            pltpu.VMEM(wide, BF16), pltpu.VMEM(wide, BF16), pltpu.VMEM(wide, BF16),
            pltpu.VMEM(narrow, BF16), pltpu.VMEM(narrow, BF16),
            pltpu.VMEM((heads, rows), F32), pltpu.VMEM((2, heads, half), F32), pltpu.VMEM((2, heads, half), F32),
            *[pltpu.VMEM(narrow, BF16) for _ in range(2 * steps)],
            pltpu.VMEM((steps, 4, half, HD), BF16), pltpu.VMEM((2,) + narrow, F32),
            pltpu.VMEM((3 * half, width), BF16), pltpu.VMEM((2 * half, width), BF16),
            pltpu.VMEM(((3 + 2 * steps) * half, width), BF16),
            pltpu.VMEM((2 * HD, (3 + 2 * steps) * half), BF16),
            pltpu.VMEM(wide, BF16),
            dma((6,)), dma((steps,)), dma((steps,)), dma((steps,)), dma((steps,)),
            dma((2 * steps,)), dma((2 * steps,)), dma((heads // 2 + 1,)),
        ],
        compiler_params=pltpu.CompilerParams(
            collective_id=0, has_side_effects=True, vmem_limit_bytes=60 * 1024 * 1024
        ),
        cost_estimate=pl.CostEstimate(
            flops=2 * 5 * 9 * heads * half * half * HD, bytes_accessed=4 * rows * width * 2,
            transcendentals=9 * heads * half * half,
        ),
    )(
        span_table.T, queries.reshape(wide), key_rows.reshape(narrow), value_rows.reshape(narrow),
        out_grad.reshape(wide), outputs.reshape(wide), log_sum,
    )
    dq, dk, dv = pl.pallas_call(
        place,
        out_shape=(
            jax.ShapeDtypeStruct(wide, BF16),
            jax.ShapeDtypeStruct(narrow, F32),
            jax.ShapeDtypeStruct(narrow, F32),
        ),
        in_specs=[any_spec] * 3,
        out_specs=[any_spec] * 3,
        scratch_shapes=[
            pltpu.VMEM(wide, BF16), pltpu.VMEM((2,) + narrow, F32), pltpu.VMEM((steps, 4, half, HD), BF16),
            pltpu.VMEM(narrow, F32), pltpu.VMEM(narrow, F32), dma((6,)), dma((6,)),
        ],
        compiler_params=pltpu.CompilerParams(vmem_limit_bytes=60 * 1024 * 1024),
    )(dq, own, parts)
    return dq.reshape(rows, width), dk.reshape(rows, HD), dv.reshape(rows, HD)


def solution(mesh):
    rows = P(("outer", "inner"), None)
    return jax.shard_map(
        functools.partial(per_device, mesh.shape["outer"], mesh.shape["inner"]),
        mesh=mesh,
        in_specs=(rows, rows, rows, rows, rows, P(None, ("outer", "inner")), P()),
        out_specs=(rows, rows, rows),
        check_vma=False,
    )
```
